32 devices in a mesh: gx: 4 (over y, x), gy: 8 (over z, core).
Axes of the slice: x: 2, y: 2, z: 4, core: 2. Of those that a mesh axis runs over, the one named last changes fastest.
Arguments:
- picture_embeds: bfloat16 [32768, 1152], P(('gx', 'gy')), may hold values from -6 to 6
- motion_embeds: bfloat16 [32768, 1152], P(('gx', 'gy')), may hold values from -6 to 6
- match_indices: int32 [32, 1024], P(('gx', 'gy')), may hold values from 0 to 1023, each once within a row
- sharpness_coefficient: float32 [1], replicated, may hold values from 0.04 to 0.12
- additive_shift: float32 [1], replicated, may hold values from -3 to -1
- precision_gain: float32 [1], replicated, may hold values from 16384 to 65536
Outputs:
- grad_image: bfloat16 [32768, 1152], P(('gx', 'gy'))
- grad_sensor: bfloat16 [32768, 1152], P(('gx', 'gy'))
The draws below stay inside these ranges and needn't reach their ends.
Inputs may be any that keep to these rules, and one draw needn't show every extreme that they name: Each row of match_indices is a permutation of 0 to 1023.
All inputs are finite; a program needn't handle non-finite values.
Results may differ from the reference program's by a relative error of at most 0.0038.
Values may be sent and summed in bfloat16 or wider, within the bound.
A program may use at most 128 MiB of HBM per device.

```python
import math
import jax
import jax.numpy as jnp
from jax import lax

D = 1152
TILE_HEIGHT = 1024
BLOCKS = 32
TOTAL = 32768


def shard_levels(own_key, shape, cuts, low, high):
    gain = 1.0
    for dim, shards_of in cuts:
        steps = jax.random.uniform(jax.random.fold_in(jax.random.fold_in(own_key, 6), dim), (shards_of,), jnp.float32, low / len(cuts), high / len(cuts))
        gain = gain * jnp.repeat(jnp.exp(steps), shape[dim] // shards_of).reshape((-1,) + (1,) * (len(shape) - 1 - dim))
    return gain


def bell_draw(stream_key, dims, deviation, reach, shards=(), kind=jnp.bfloat16):
    values = jax.random.normal(stream_key, dims, jnp.float32) * deviation
    if len(shards) > 0:
        values = shard_levels(stream_key, dims, shards, -0.22, 0.18) * values
    return jnp.clip(values, min=-reach, max=reach).astype(kind)


def setup_inputs(seed: int = 0) -> dict:
    splits = jax.random.split(jax.random.key(seed), 7)
    picture_embeds = bell_draw(splits[0], (TOTAL, D), 1.0, 6.0, ((0, 32),))
    motion_embeds = bell_draw(splits[1], (TOTAL, D), 1.0, 6.0, ((0, 32),))
    match_indices = jax.vmap(lambda own: jax.random.permutation(own, TILE_HEIGHT))(jax.random.split(splits[2], BLOCKS)).reshape((BLOCKS, TILE_HEIGHT)).astype(jnp.int32)
    sharpness_coefficient = jnp.clip(jax.random.uniform(splits[3], (1,), jnp.float32, 0.04, 0.12), 0.04, 0.12)
    additive_shift = jnp.clip(jax.random.uniform(splits[4], (1,), jnp.float32, -3.0, -1.0), -3.0, -1.0)
    precision_gain = jnp.clip(jnp.exp(jax.random.uniform(splits[5], (1,), jnp.float32, math.log(16384.0), math.log(65536.0))), 16384.0, 65536.0)
    return {"picture_embeds": picture_embeds, "motion_embeds": motion_embeds, "match_indices": match_indices, "sharpness_coefficient": sharpness_coefficient, "additive_shift": additive_shift, "precision_gain": precision_gain}


window_offsets = (-1, 0, 1, 2)


def reference(picture_embeds, motion_embeds, match_indices, sharpness_coefficient, additive_shift, precision_gain):
    tile_total = match_indices.shape[0]
    width = picture_embeds.shape[1]
    picture_tile = picture_embeds.reshape(tile_total, TILE_HEIGHT, width).astype(jnp.float32)
    sensors = motion_embeds.reshape(tile_total, TILE_HEIGHT, width).astype(jnp.float32)
    objective_coefficient = precision_gain[0] * sharpness_coefficient[0] / (tile_total * TILE_HEIGHT)
    columns = jnp.arange(TILE_HEIGHT, dtype=jnp.int32)
    match_target = (match_indices[:, :, None] == columns[None, None, :]).astype(jnp.float32)
    grad_img = jnp.zeros(picture_tile.shape, jnp.float32)
    grad_sen = jnp.zeros(picture_tile.shape, jnp.float32)
    for offset in window_offsets:
        companion_tile = jnp.roll(sensors, -offset, axis=0)
        similarity_grid = sharpness_coefficient[0] * jnp.einsum('wrn,wun->wru', picture_tile, companion_tile) + additive_shift[0]
        logistic_derivative = jax.nn.sigmoid(similarity_grid)
        if offset == 0:
            logistic_derivative = logistic_derivative - match_target
        rounded = lax.optimization_barrier((objective_coefficient * logistic_derivative).astype(jnp.bfloat16))
        weights = rounded.astype(jnp.float32)
        grad_img = grad_img + jnp.einsum('prc,pcd->prd', weights, companion_tile)
        terms = jnp.einsum('prc,prd->pcd', weights, picture_tile)
        grad_sen = grad_sen + jnp.roll(terms, offset, axis=0)
    grad_image = grad_img.reshape(tile_total * TILE_HEIGHT, width).astype(jnp.bfloat16)
    grad_sensor = grad_sen.reshape(tile_total * TILE_HEIGHT, width).astype(jnp.bfloat16)
    return (grad_image, grad_sensor)
```

```python
import jax
import jax.numpy as jnp
from jax import lax
from jax.sharding import PartitionSpec as P

AXES = ("gx", "gy")


def shifted(value, by):
    n = lax.axis_size(AXES)
    return lax.ppermute(value, AXES, [(i, (i + by) % n) for i in range(n)])


def swapped(value):
    n = lax.axis_size(AXES)
    return lax.ppermute(value, AXES, [(i, i ^ 1) for i in range(n)])


def pair_weights(own, other, sharpness, shift, objective, target):
    logits = lax.dot_general(
        own, other, (((1,), (1,)), ((), ())), preferred_element_type=jnp.float32
    )
    slope = jax.nn.sigmoid(sharpness[0] * logits + shift[0])
    if target is not None:
        slope = slope - target
    return (objective * slope).astype(jnp.bfloat16)


def per_device(image, sensor, match, sharpness, shift, gain):
    rows = image.shape[0]
    n = lax.axis_size(AXES)
    objective = gain[0] * sharpness[0] / (rows * n)
    first_core = lax.rem(lax.axis_index(AXES), 2) == 0
    sensor_two = shifted(sensor, -2)
    image_two = shifted(image, 2)
    sensor_before = shifted(sensor, 1)
    image_after = shifted(image, -1)
    sensor_after = swapped(jnp.where(first_core, sensor_two, sensor))
    image_before = swapped(jnp.where(first_core, image, image_two))
    columns = jnp.arange(rows, dtype=jnp.int32)
    target = (match[0][:, None] == columns[None, :]).astype(jnp.float32)
    weights = pair_weights(image, sensor, sharpness, shift, objective, target)

    def dot(a, b):
        return jnp.dot(a, b, preferred_element_type=jnp.float32)

    grad_image = dot(weights, sensor)
    grad_sensor = lax.dot_general(
        weights, image, (((0,), (0,)), ((), ())), preferred_element_type=jnp.float32
    )
    for other in (sensor_before, sensor_after, sensor_two):
        grad_image += dot(pair_weights(image, other, sharpness, shift, objective, None), other)
    for other in (image_after, image_before, image_two):
        grad_sensor += dot(pair_weights(sensor, other, sharpness, shift, objective, None), other)
    return grad_image.astype(jnp.bfloat16), grad_sensor.astype(jnp.bfloat16)


def solution(mesh):
    rows = P(AXES, None)
    return jax.shard_map(
        per_device,
        mesh=mesh,
        in_specs=(rows, rows, rows, P(), P(), P()),
        out_specs=(rows, rows),
        check_vma=False,
    )
```

```python
import functools

import jax
import jax.numpy as jnp
from jax import lax
from jax.experimental import pallas as pl
from jax.experimental.pallas import tpu as pltpu
from jax.sharding import PartitionSpec as P

AXES = ("gx", "gy")
MESH = pl.DeviceIdType.MESH
SIB_SENSOR, SIB_IMAGE, TWO_SENSOR, TWO_IMAGE, FORWARDED, FAR = range(6)
CHUNK = 256
TILE = 512


def kernel(
    sizes,
    image_hbm,
    sensor_hbm,
    match_ref,
    sharpness_ref,
    shift_ref,
    gain_ref,
    grad_image_hbm,
    grad_sensor_hbm,
    own,
    got,
    acc,
    stage,
    load_sem,
    store_sem,
    send_sem,
    recv_sem,
):
    per_row, total_devices = sizes[1], sizes[0] * sizes[1]
    rows = own.shape[1]
    chunks, tiles = rows // CHUNK, rows // TILE
    me = lax.axis_index("gx") * per_row + lax.axis_index("gy")
    core = lax.rem(me, 2)

    def place(index):
        index = lax.rem(index + total_devices, total_devices)
        return (lax.div(index, per_row), lax.rem(index, per_row))

    sibling = place(me + 1 - 2 * core)
    above, below = place(me + 2), place(me - 2)
    beside = place(me - 1 + 2 * core)

    loads = [
        pltpu.make_async_copy(image_hbm, own.at[0], load_sem.at[0]),
        pltpu.make_async_copy(sensor_hbm, own.at[1], load_sem.at[1]),
    ]
    for load in loads:
        load.start()
    barrier = pltpu.get_barrier_semaphore()
    for device in (sibling, above, below, beside):
        pl.semaphore_signal(barrier, inc=1, device_id=device, device_id_type=MESH)
    pl.semaphore_wait(barrier, 4)
    for load in loads:
        load.wait()

    def part(c):
        return pl.ds(pl.multiple_of(c * CHUNK, CHUNK), CHUNK)

    def copy(role, c):
        source, device = {
            SIB_SENSOR: (lambda: own.at[1, part(c)], sibling),
            SIB_IMAGE: (lambda: own.at[0, part(c)], sibling),
            TWO_SENSOR: (lambda: own.at[1, part(c)], below),
            TWO_IMAGE: (lambda: own.at[0, part(c)], above),
            FORWARDED: (lambda: got.at[TWO_SENSOR + core, part(c)], sibling),
            FAR: (lambda: own.at[core, part(c)], beside),
        }[role]
        return pltpu.make_async_remote_copy(
            src_ref=source(),
            dst_ref=got.at[role, part(c)],
            send_sem=send_sem.at[role, c],
            recv_sem=recv_sem.at[role, c],
            device_id=device,
            device_id_type=MESH,
        )

    def each(count, body):
        lax.fori_loop(0, count, lambda i, _: (body(i), 0)[1], 0)

    def send_far(c):
        for role in (TWO_SENSOR, TWO_IMAGE, FAR):
            copy(role, c).start()

    def send_near(c):
        for role in (SIB_SENSOR, SIB_IMAGE):
            copy(role, c).start()

    each(chunks, send_far)
    each(chunks, send_near)

    sharpness, shift = sharpness_ref[0], shift_ref[0]
    objective = gain_ref[0] * sharpness / (rows * total_devices)

    def slope(mine, other):
        logits = lax.dot_general(
            mine, other, (((1,), (1,)), ((), ())), preferred_element_type=jnp.float32
        )
        return jax.nn.sigmoid(sharpness * logits + shift)

    def own_pair(c):
        other = own[0, part(c)]
        matched = match_ref[:, part(c)]

        def tile(t):
            span = pl.ds(pl.multiple_of(t * TILE, TILE), TILE)
            mine = own[1, span]
            column = t * TILE + lax.broadcasted_iota(jnp.int32, (TILE, CHUNK), 0)
            positive = (column == matched).astype(jnp.float32)
            weights = (objective * (slope(mine, other) - positive)).astype(jnp.bfloat16)
            term = jnp.dot(weights, other, preferred_element_type=jnp.float32)
            back = lax.dot_general(
                weights, mine, (((0,), (0,)), ((), ())), preferred_element_type=jnp.float32
            )

            acc[1, span] += term
            acc[0, part(c)] += back

        each(tiles, tile)

    acc[...] = jnp.zeros_like(acc)
    each(chunks, own_pair)

    def add_pair(side, role, c):
        other_at = part(c)

        def tile(t):
            span = pl.ds(pl.multiple_of(t * TILE, TILE), TILE)
            other = got[role, other_at]
            weights = (objective * slope(own[side, span], other)).astype(jnp.bfloat16)
            acc[side, span] += jnp.dot(weights, other, preferred_element_type=jnp.float32)

        each(tiles, tile)

    def near(c):
        for side, role in ((0, SIB_SENSOR), (1, SIB_IMAGE)):
            copy(role, c).wait_recv()
            add_pair(side, role, c)

    each(chunks, near)

    def remote(c):
        for role in (TWO_SENSOR, TWO_IMAGE):
            copy(role, c).wait_recv()
        copy(FORWARDED, c).start()
        add_pair(0, TWO_SENSOR, c)
        add_pair(1, TWO_IMAGE, c)
        copy(FAR, c).wait_recv()
        add_pair(core, FAR, c)
        copy(FORWARDED, c).wait_recv()
        add_pair(1 - core, FORWARDED, c)

    each(chunks, remote)

    outs = (grad_image_hbm, grad_sensor_hbm)

    def store(side, t):
        span = pl.ds(pl.multiple_of(t * TILE, TILE), TILE)
        return pltpu.make_async_copy(
            stage.at[side, span], outs[side].at[span], store_sem.at[side, t]
        )

    def finish(t):
        span = pl.ds(pl.multiple_of(t * TILE, TILE), TILE)
        for side in range(2):
            stage[side, span] = acc[side, span].astype(jnp.bfloat16)
            store(side, t).start()

    each(tiles, finish)

    def sent(c):
        for role in range(6):
            copy(role, c).wait_send()

    each(chunks, sent)
    for side in range(2):
        each(tiles, functools.partial(lambda side, t: store(side, t).wait(), side))


def per_device(sizes, image, sensor, match, sharpness, shift, gain):
    rows, width = image.shape
    anywhere = pl.BlockSpec(memory_space=pl.ANY)
    scalar = pl.BlockSpec(memory_space=pltpu.SMEM)
    chunks, tiles = rows // CHUNK, rows // TILE
    return pl.pallas_call(
        functools.partial(kernel, sizes),
        out_shape=[jax.ShapeDtypeStruct((rows, width), jnp.bfloat16)] * 2,
        in_specs=[anywhere, anywhere, pl.BlockSpec(memory_space=pltpu.VMEM)] + [scalar] * 3,
        out_specs=[anywhere, anywhere],
        scratch_shapes=[
            pltpu.VMEM((2, rows, width), jnp.bfloat16),
            pltpu.VMEM((6, rows, width), jnp.bfloat16),
            pltpu.VMEM((2, rows, width), jnp.float32),
            pltpu.VMEM((2, rows, width), jnp.bfloat16),
            pltpu.SemaphoreType.DMA((2,)),
            pltpu.SemaphoreType.DMA((2, tiles)),
            pltpu.SemaphoreType.DMA((6, chunks)),
            pltpu.SemaphoreType.DMA((6, chunks)),
        ],
        compiler_params=pltpu.CompilerParams(
            collective_id=0, has_side_effects=True, vmem_limit_bytes=56 * 2**20
        ),
        cost_estimate=pl.CostEstimate(
            flops=32 * rows * rows * width,
            bytes_accessed=8 * rows * width,
            transcendentals=8 * rows * rows,
        ),
    )(image, sensor, match, sharpness, shift, gain)


def solution(mesh):
    rows = P(AXES, None)
    sizes = tuple(mesh.shape[axis] for axis in AXES)
    return jax.shard_map(
        functools.partial(per_device, sizes),
        mesh=mesh,
        in_specs=(rows, rows, rows, P(), P(), P()),
        out_specs=(rows, rows),
        check_vma=False,
    )
```

```python
import functools

import jax
import jax.numpy as jnp
from jax import lax
from jax.experimental import pallas as pl
from jax.experimental.pallas import tpu as pltpu
from jax.sharding import PartitionSpec as P

AXES = ("gx", "gy")
MESH = pl.DeviceIdType.MESH
SIB_SENSOR, SIB_IMAGE, TWO_SENSOR, TWO_IMAGE, FORWARDED, FAR = range(6)
CHUNK = 256
TILE = 512


def kernel(
    sizes,
    image_hbm,
    sensor_hbm,
    match_ref,
    sharpness_ref,
    shift_ref,
    gain_ref,
    grad_image_ref,
    grad_sensor_ref,
    own,
    got,
    acc,
    load_sem,
    send_sem,
    recv_sem,
):
    per_row, total_devices = sizes[1], sizes[0] * sizes[1]
    rows = own.shape[1]
    chunks, tiles = rows // CHUNK, rows // TILE
    me = lax.axis_index("gx") * per_row + lax.axis_index("gy")
    core = lax.rem(me, 2)

    def place(index):
        index = lax.rem(index + total_devices, total_devices)
        return (lax.div(index, per_row), lax.rem(index, per_row))

    sibling = place(me + 1 - 2 * core)
    above, below = place(me + 2), place(me - 2)
    beside = place(me - 1 + 2 * core)

    loads = [
        pltpu.make_async_copy(image_hbm, own.at[0], load_sem.at[0]),
        pltpu.make_async_copy(sensor_hbm, own.at[1], load_sem.at[1]),
    ]
    for load in loads:
        load.start()
    barrier = pltpu.get_barrier_semaphore()
    for device in (sibling, above, below, beside):
        pl.semaphore_signal(barrier, inc=1, device_id=device, device_id_type=MESH)
    pl.semaphore_wait(barrier, 4)
    for load in loads:
        load.wait()

    def part(c):
        return pl.ds(pl.multiple_of(c * CHUNK, CHUNK), CHUNK)

    def copy(role, c):
        source, device = {
            SIB_SENSOR: (lambda: own.at[1, part(c)], sibling),
            SIB_IMAGE: (lambda: own.at[0, part(c)], sibling),
            TWO_SENSOR: (lambda: own.at[1, part(c)], below),
            TWO_IMAGE: (lambda: own.at[0, part(c)], above),
            FORWARDED: (lambda: got.at[TWO_SENSOR + core, part(c)], sibling),
            FAR: (lambda: own.at[core, part(c)], beside),
        }[role]
        return pltpu.make_async_remote_copy(
            src_ref=source(),
            dst_ref=got.at[role, part(c)],
            send_sem=send_sem.at[role, c],
            recv_sem=recv_sem.at[role, c],
            device_id=device,
            device_id_type=MESH,
        )

    def each(count, body):
        lax.fori_loop(0, count, lambda i, _: (body(i), 0)[1], 0)

    def send_far(c):
        for role in (TWO_SENSOR, TWO_IMAGE):
            copy(role, c).start()

    def send_near(c):
        for role in (SIB_SENSOR, SIB_IMAGE):
            copy(role, c).start()

    each(chunks, send_far)
    each(chunks, lambda c: copy(FAR, c).start())
    each(chunks, send_near)

    sharpness, shift = sharpness_ref[0], shift_ref[0]
    objective = gain_ref[0] * sharpness / (rows * total_devices)

    def slope(mine, other):
        logits = lax.dot_general(
            mine, other, (((1,), (1,)), ((), ())), preferred_element_type=jnp.float32
        )
        return jax.nn.sigmoid(sharpness * logits + shift)

    def tile_rows(t):
        return pl.ds(pl.multiple_of(t * TILE, TILE), TILE)

    def own_pair(c):
        other = own[0, part(c)]
        matched = match_ref[:, part(c)]

        def tile(t):
            span = pl.ds(pl.multiple_of(t * TILE, TILE), TILE)
            mine = own[1, span]
            column = t * TILE + lax.broadcasted_iota(jnp.int32, (TILE, CHUNK), 0)
            positive = (column == matched).astype(jnp.float32)
            weights = (objective * (slope(mine, other) - positive)).astype(jnp.bfloat16)
            term = jnp.dot(weights, other, preferred_element_type=jnp.float32)
            back = lax.dot_general(
                weights, mine, (((0,), (0,)), ((), ())), preferred_element_type=jnp.float32
            )

            acc[1, span] += term
            acc[0, part(c)] += back

        each(tiles, tile)

    acc[...] = jnp.zeros_like(acc)
    each(chunks, own_pair)

    def add_pair(side, role, c, last=False):
        def tile(t):
            span = tile_rows(t)
            other = got[role, part(c)]
            weights = (objective * slope(own[side, span], other)).astype(jnp.bfloat16)
            term = jnp.dot(weights, other, preferred_element_type=jnp.float32)
            if last:
                total = (acc[side, span] + term).astype(jnp.bfloat16)
                for out_side, out in enumerate((grad_image_ref, grad_sensor_ref)):

                    @pl.when(side == out_side)
                    def _(out=out):
                        out[span] = total

            else:
                acc[side, span] += term

        each(tiles, tile)

    def near(c):
        for side, role in ((0, SIB_SENSOR), (1, SIB_IMAGE)):
            copy(role, c).wait_recv()
            add_pair(side, role, c)

    each(chunks, near)

    def shared(c, last=False):
        copy(FORWARDED, c).wait_recv()
        add_pair(1 - core, FORWARDED, c, last)

    def remote(c):
        for role in (TWO_SENSOR, TWO_IMAGE):
            copy(role, c).wait_recv()
        copy(FORWARDED, c).start()
        add_pair(0, TWO_SENSOR, c)
        add_pair(1, TWO_IMAGE, c)

        @pl.when(c > 0)
        def _():
            shared(c - 1)

    each(chunks, remote)
    shared(chunks - 1, True)

    def far(c, last=False):
        copy(FAR, c).wait_recv()
        add_pair(core, FAR, c, last)

    each(chunks - 1, far)
    far(chunks - 1, True)

    def sent(c):
        for role in range(6):
            copy(role, c).wait_send()

    each(chunks, sent)


def per_device(sizes, image, sensor, match, sharpness, shift, gain):
    rows, width = image.shape
    anywhere = pl.BlockSpec(memory_space=pl.ANY)
    scalar = pl.BlockSpec(memory_space=pltpu.SMEM)
    chunks = rows // CHUNK
    return pl.pallas_call(
        functools.partial(kernel, sizes),
        out_shape=[pltpu.VMEM((rows, width), jnp.bfloat16)] * 2,
        in_specs=[anywhere, anywhere, pl.BlockSpec(memory_space=pltpu.VMEM)] + [scalar] * 3,
        out_specs=[pl.BlockSpec(memory_space=pltpu.VMEM)] * 2,
        scratch_shapes=[
            pltpu.VMEM((2, rows, width), jnp.bfloat16),
            pltpu.VMEM((6, rows, width), jnp.bfloat16),
            pltpu.VMEM((2, rows, width), jnp.float32),
            pltpu.SemaphoreType.DMA((2,)),
            pltpu.SemaphoreType.DMA((6, chunks)),
            pltpu.SemaphoreType.DMA((6, chunks)),
        ],
        compiler_params=pltpu.CompilerParams(
            collective_id=0, has_side_effects=True, vmem_limit_bytes=48 * 2**20
        ),
        cost_estimate=pl.CostEstimate(
            flops=32 * rows * rows * width,
            bytes_accessed=8 * rows * width,
            transcendentals=8 * rows * rows,
        ),
    )(image, sensor, match, sharpness, shift, gain)


def solution(mesh):
    rows = P(AXES, None)
    sizes = tuple(mesh.shape[axis] for axis in AXES)
    return jax.shard_map(
        functools.partial(per_device, sizes),
        mesh=mesh,
        in_specs=(rows, rows, rows, P(), P(), P()),
        out_specs=(rows, rows),
        check_vma=False,
    )
```
